32 devices in a mesh: dp: 2 (over core), ctx: 2 (over y), feat: 8 (over z, x).
Axes of the slice: x: 2, y: 2, z: 4, core: 2. Of those that a mesh axis runs over, the one named last changes fastest.
Arguments:
- out_grads: bfloat16 [512, 28672], P(('dp', 'ctx'), 'feat'), may hold values from -6 to 6
- acts: bfloat16 [512, 8192], P(('dp', 'ctx'), 'feat'), may hold values from -6 to 6
- domain_ids: int32 [512], P(('dp', 'ctx')), may hold values from 0 to 7
- domain_weights: int32 [8], replicated, may hold values from 1 to 4
Outputs:
- grad_factor: bfloat16 [28672, 28672], P(('dp', 'ctx'), 'feat')
- act_factor: bfloat16 [8192, 8192], P(('dp', 'ctx'), 'feat')
The draws below stay inside these ranges and needn't reach their ends.
All inputs are finite; a program needn't handle non-finite values.
Results may differ from the reference program's by a relative error of at most 0.003.
Values may be sent and summed in bfloat16 or wider, within the bound.
A program may use at most 128 MiB of HBM per device.

```python
import jax
import jax.numpy as jnp
from jax import lax

D = 8192
FF = 28672
DOMAINS = 8
TOKENS = 512


def set_ends(array, rng, low, top_value):
    longest = array.shape.index(max(array.shape))
    spots = []
    for shift in (0, 1):
        where = [jax.random.randint(jax.random.fold_in(rng, axis), (), 0, length) for axis, length in enumerate(array.shape)]
        where[longest] = (where[longest] + shift) % array.shape[longest]
        spots.append(tuple(where))
    return array.at[spots[0]].set(low).at[spots[1]].set(top_value)


def spiked(result, own_key, source, target, parts, factor):
    def block_of(position):
        return (jnp.arange(result.shape[position]) // (result.shape[position] // parts)).reshape((-1,) + (1,) * (result.ndim - 1 - position))

    near = jax.random.permutation(own_key, parts)[block_of(target)]
    second = (block_of(target) + parts // 2) % parts
    return jnp.where((block_of(source) == near) | (block_of(source) == second), factor * result, result)


def block_levels(own_key, dims, pieces, smallest, largest):
    factor_of = 1.0
    for dim, shards_of in pieces:
        draws = jax.random.uniform(jax.random.fold_in(jax.random.fold_in(own_key, 6), dim), (shards_of,), jnp.float32, smallest / len(pieces), largest / len(pieces))
        factor_of = factor_of * jnp.repeat(jnp.exp(draws), dims[dim] // shards_of).reshape((-1,) + (1,) * (len(dims) - 1 - dim))
    return factor_of


def scatter_about(own_key, extent, scale, reach, cuts=(), kind=jnp.bfloat16):
    level = block_levels(own_key, extent, cuts, -0.22, 0.18) if cuts else 1.0
    entries = jax.random.normal(own_key, extent, jnp.float32) * scale * level
    return jnp.minimum(jnp.maximum(entries, -reach), reach).astype(kind)


def bell_draw_with(rng, dims, spread, limit, split, heavy, held_as=jnp.bfloat16):
    drawn = spread * jax.random.normal(rng, dims, jnp.float32)
    if split:
        drawn = drawn * block_levels(rng, dims, split, -0.22, 0.18)
    return jnp.clip(spiked(drawn, jax.random.fold_in(rng, 3), *heavy), -limit, limit).astype(held_as)


def setup_inputs(seed: int = 0) -> dict:
    streams_of = jax.random.split(jax.random.key(seed), 5)
    out_grads = bell_draw_with(streams_of[0], (TOKENS, FF), 1.0, 6.0, ((0, 4), (1, 8)), (0, 1, 8, 2.0))
    acts = scatter_about(streams_of[1], (TOKENS, D), 1.0, 6.0, ((0, 4), (1, 8)))
    domain_ids = set_ends(jax.random.randint(streams_of[2], (TOKENS,), 0, DOMAINS), jax.random.fold_in(streams_of[2], 1), 0, DOMAINS - 1).astype(jnp.int32)
    domain_weights = set_ends(jax.random.randint(streams_of[3], (DOMAINS,), 1, 5), jax.random.fold_in(streams_of[3], 1), 1, 4).astype(jnp.int32)
    return {"out_grads": out_grads, "acts": acts, "domain_ids": domain_ids, "domain_weights": domain_weights}


def gram_blocks(rows, weighted, inv_count):
    width = rows.shape[1]
    block_width = 512 if width % 512 == 0 else width
    blocks = width // block_width
    stacked = rows.reshape(rows.shape[0], blocks, block_width).transpose(1, 0, 2)

    def one_block(piece):
        product = jnp.dot(piece.T, weighted, preferred_element_type=jnp.float32)
        return (product * inv_count).astype(jnp.bfloat16)

    return lax.map(one_block, stacked).reshape(width, width)


def reference(out_grads, acts, domain_ids, domain_weights):
    token_weight = domain_weights[domain_ids].astype(jnp.float32)
    weighted_grads = (token_weight[:, None] * out_grads.astype(jnp.float32)).astype(jnp.bfloat16)
    weighted_acts = (token_weight[:, None] * acts.astype(jnp.float32)).astype(jnp.bfloat16)
    inv_count = 1.0 / TOKENS
    grad_factor = gram_blocks(out_grads, weighted_grads, inv_count)
    act_factor = gram_blocks(acts, weighted_acts, inv_count)
    return grad_factor, act_factor
```

```python
import functools

import jax
import jax.numpy as jnp
from jax import lax
from jax.experimental import pallas as pl
from jax.experimental.pallas import tpu as pltpu
from jax.sharding import PartitionSpec as P

MESH = pl.DeviceIdType.MESH
LANES = 128
ROW_STEP = 32
VMEM_LIMIT = 56 * 1024 * 1024


def gather_kernel(sizes, width, mine_ref, cols_ref, rows_ref,
                  own_sem, fill_sem, swap_send, swap_recv, down_send, up_send, flow_recv,
                  side_send, side_recv):
    n_dp, n_ctx, n_feat = sizes
    group = n_dp * n_ctx
    ratio = n_feat // group
    tokens = mine_ref.shape[0]
    pieces = tokens // ROW_STEP
    steps = group * pieces

    dp, ctx, feat = lax.axis_index("dp"), lax.axis_index("ctx"), lax.axis_index("feat")
    me = dp * n_ctx + ctx
    stage, lane = feat // ratio, feat % ratio

    def in_group(other):
        return {"dp": other // n_ctx, "ctx": other % n_ctx, "feat": feat}

    def on_feat(other):
        return {"dp": dp, "ctx": ctx, "feat": other}

    mates = [lax.rem(me + shift, group) for shift in range(1, group)]
    sides = [stage * ratio + lax.rem(lane + shift, ratio) for shift in range(1, ratio)]
    has_down, has_up = stage > 0, stage < group - 1

    barrier = pltpu.get_barrier_semaphore()
    for mate in mates:
        pl.semaphore_signal(barrier, inc=1, device_id=in_group(mate), device_id_type=MESH)
    for side in sides:
        pl.semaphore_signal(barrier, inc=1, device_id=on_feat(side), device_id_type=MESH)

    @pl.when(has_down)
    def _():
        pl.semaphore_signal(barrier, inc=1, device_id=on_feat(feat - ratio), device_id_type=MESH)

    @pl.when(has_up)
    def _():
        pl.semaphore_signal(barrier, inc=1, device_id=on_feat(feat + ratio), device_id_type=MESH)

    near = has_down.astype(jnp.int32) + has_up.astype(jnp.int32)
    pl.semaphore_wait(barrier, len(mates) + len(sides) + near)

    my_rows = cols_ref.at[pl.ds(pl.multiple_of(me * tokens, tokens), tokens)]
    own = pltpu.make_async_copy(mine_ref, my_rows, own_sem)
    own.start()

    def swap(shift):
        return pltpu.make_async_remote_copy(
            src_ref=mine_ref, dst_ref=my_rows,
            send_sem=swap_send.at[shift], recv_sem=swap_recv.at[group - shift],
            device_id=in_group(lax.rem(me + shift, group)), device_id_type=MESH)

    def swapped(shift):
        block = lax.rem(me + shift, group)
        rows = cols_ref.at[pl.ds(pl.multiple_of(block * tokens, tokens), tokens)]
        return pltpu.make_async_remote_copy(
            src_ref=mine_ref, dst_ref=rows,
            send_sem=swap_send.at[shift], recv_sem=swap_recv.at[shift],
            device_id=in_group(block), device_id_type=MESH)

    half = group // 2
    order = [(k % 2) * half + k // 2 for k in range(group)] if group % 2 == 0 else list(range(group))
    for shift in order[1:]:
        swap(shift).start()
    own.wait()

    is_root = stage == me
    is_flow = jnp.logical_not(is_root)
    send_down = jnp.logical_and(stage <= me, has_down)
    send_up = jnp.logical_and(stage >= me, has_up)

    def block_of(k):
        shift = (k % 2) * half + k // 2 if group % 2 == 0 else k
        return shift, lax.rem(me + shift, group)

    def span(q):
        shift, block = block_of(q // pieces)
        start = block * tokens + (q % pieces) * ROW_STEP
        return pl.ds(pl.multiple_of(start, ROW_STEP), ROW_STEP)

    def from_root(q):
        return cols_ref.at[span(q), pl.ds(0, width)]

    def landed(q, which):
        return rows_ref.at[which, span(q)]

    def remote(src, q, which, send, recv, target):
        return pltpu.make_async_remote_copy(
            src_ref=src, dst_ref=landed(q, which), send_sem=send, recv_sem=recv,
            device_id=on_feat(target), device_id_type=MESH)

    def fill(k):
        _, block = block_of(k)
        rows = pl.ds(pl.multiple_of(block * tokens, tokens), tokens)
        return pltpu.make_async_copy(
            cols_ref.at[rows, pl.ds(0, width)], rows_ref.at[lane, rows], fill_sem.at[k])

    def send_on(src, q):
        @pl.when(send_down)
        def _():
            remote(src, q, lane, down_send.at[q], flow_recv.at[q], feat - ratio).start()

        @pl.when(send_up)
        def _():
            remote(src, q, lane, up_send.at[q], flow_recv.at[q], feat + ratio).start()

        for i, side in enumerate(sides):
            remote(src, q, lane, side_send.at[i, q], side_recv.at[ratio - 2 - i, q], side).start()

    @pl.when(is_root)
    def _():
        def body(q, carry):
            k = q // pieces

            @pl.when(jnp.logical_and(q % pieces == 0, k > 0))
            def _():
                shift, _ = block_of(k)
                swapped(shift).wait_recv()

            @pl.when(q % pieces == 0)
            def _():
                fill(k).start()

            send_on(from_root(q), q)
            return carry

        lax.fori_loop(0, steps, body, 0)

        def settle(k, carry):
            fill(k).wait()
            return carry

        lax.fori_loop(0, group, settle, 0)

    @pl.when(is_flow)
    def _():
        def body(q, carry):
            remote(landed(q, lane), q, lane, down_send.at[q], flow_recv.at[q], feat).wait_recv()
            send_on(landed(q, lane), q)
            return carry

        lax.fori_loop(0, steps, body, 0)
        for shift in order[1:]:
            swapped(shift).wait_recv()

    def drain(q, carry):
        here = landed(q, lane)
        for i in range(ratio - 1):
            other = lax.rem(lane + i + 1, ratio)
            remote(here, q, other, side_send.at[i, q], side_recv.at[i, q], feat).wait_recv()
            remote(here, q, lane, side_send.at[i, q], side_recv.at[i, q], feat).wait_send()

        @pl.when(send_down)
        def _():
            remote(here, q, lane, down_send.at[q], flow_recv.at[q], feat).wait_send()

        @pl.when(send_up)
        def _():
            remote(here, q, lane, up_send.at[q], flow_recv.at[q], feat).wait_send()

        return carry

    lax.fori_loop(0, steps, drain, 0)
    for shift in order[1:]:
        swap(shift).wait_send()


def gather_tiles(mine, sizes, width):
    n_dp, n_ctx, n_feat = sizes
    group = n_dp * n_ctx
    ratio = n_feat // group
    tokens = mine.shape[0]
    steps = group * (tokens // ROW_STEP)
    dma = pltpu.SemaphoreType.DMA
    return pl.pallas_call(
        functools.partial(gather_kernel, sizes, width),
        out_shape=(
            jax.ShapeDtypeStruct((group * tokens, mine.shape[1]), mine.dtype),
            jax.ShapeDtypeStruct((ratio, group * tokens, width), mine.dtype),
        ),
        in_specs=[pl.BlockSpec(memory_space=pl.ANY)],
        out_specs=(pl.BlockSpec(memory_space=pl.ANY), pl.BlockSpec(memory_space=pl.ANY)),
        scratch_shapes=[
            dma, dma((group,)), dma((group,)), dma((group,)),
            dma((steps,)), dma((steps,)), dma((steps,)),
            dma((max(ratio - 1, 1), steps)), dma((max(ratio - 1, 1), steps)),
        ],
        compiler_params=pltpu.CompilerParams(
            collective_id=0, has_side_effects=True, vmem_limit_bytes=VMEM_LIMIT),
        name="gather_tiles",
    )(mine)


def gram_kernel(grad_steps, wide, inv_count, cols_ref, rows_ref, grad_ref, act_ref, weighted, turned):
    step = pl.program_id(0)
    both = weighted.shape[1]
    tile = grad_ref.shape[0]

    @pl.when(step == 0)
    def _():
        slab = 64

        def weigh(i, carry):
            at = pl.ds(pl.multiple_of(i * slab, slab), slab)
            scale = cols_ref[at, pl.ds(both, LANES)].astype(jnp.float32)[:, :1]
            weighted[at, :] = (cols_ref[at, pl.ds(0, both)].astype(jnp.float32) * scale).astype(jnp.bfloat16)
            return carry

        lax.fori_loop(0, weighted.shape[0] // slab, weigh, 0)

    turned[...] = rows_ref[0].T

    def tiles(out_ref, offset):
        chunk = tile if out_ref.shape[1] % tile == 0 else LANES
        for n in range(out_ref.shape[1] // chunk):
            total = jnp.dot(turned[...], weighted[:, pl.ds(offset + n * chunk, chunk)],
                            preferred_element_type=jnp.float32)
            out_ref[:, pl.ds(n * chunk, chunk)] = (total * inv_count).astype(jnp.bfloat16)

    @pl.when(step < grad_steps)
    def _():
        tiles(grad_ref, 0)

    @pl.when(step >= grad_steps)
    def _():
        tiles(act_ref, wide)


def gram(cols, rows, wide, narrow, inv_count):
    ratio, tokens, both = rows.shape
    tile = next(t for t in (512, 256, 128) if wide % t == 0 and narrow % t == 0)
    grad_tiles, act_tiles = wide // tile, narrow // tile
    grad_steps, act_steps = ratio * grad_tiles, ratio * act_tiles

    def row_block(i):
        j = jnp.maximum(i - grad_steps, 0)
        late = i >= grad_steps
        return (jnp.where(late, j // act_tiles, i // grad_tiles), 0,
                jnp.where(late, grad_tiles + j % act_tiles, i % grad_tiles))

    return pl.pallas_call(
        functools.partial(gram_kernel, grad_steps, wide, inv_count),
        grid=(grad_steps + act_steps,),
        out_shape=(
            jax.ShapeDtypeStruct((ratio * wide, wide), jnp.bfloat16),
            jax.ShapeDtypeStruct((ratio * narrow, narrow), jnp.bfloat16),
        ),
        in_specs=[
            pl.BlockSpec(cols.shape, lambda i: (0, 0)),
            pl.BlockSpec((1, tokens, tile), row_block),
        ],
        out_specs=(
            pl.BlockSpec((tile, wide), lambda i: (jnp.minimum(i, grad_steps - 1), 0)),
            pl.BlockSpec((tile, narrow), lambda i: (jnp.maximum(i - grad_steps, 0), 0)),
        ),
        scratch_shapes=[
            pltpu.VMEM((tokens, both), jnp.bfloat16),
            pltpu.VMEM((tile, tokens), jnp.bfloat16),
        ],
        compiler_params=pltpu.CompilerParams(vmem_limit_bytes=VMEM_LIMIT),
        cost_estimate=pl.CostEstimate(
            flops=2 * tokens * ratio * (wide * wide + narrow * narrow),
            bytes_accessed=2 * (ratio * (wide * wide + narrow * narrow) + rows.size + cols.size),
            transcendentals=0),
        name="gram",
    )(cols, rows)


def local(sizes, out_grads, acts, domain_ids, domain_weights):
    tokens, wide = out_grads.shape
    narrow = acts.shape[1]
    inv_count = 1.0 / (tokens * sizes[0] * sizes[1])
    labels = jnp.arange(domain_weights.shape[0], dtype=jnp.int32)
    match = domain_ids[:, None] == labels[None, :]
    weight = jnp.sum(jnp.where(match, domain_weights[None, :], 0), axis=1).astype(jnp.bfloat16)
    mine = jnp.concatenate(
        [out_grads, acts, jnp.broadcast_to(weight[:, None], (tokens, LANES))], axis=1)
    cols, rows = gather_tiles(mine, sizes, wide + narrow)
    return gram(cols, rows, wide, narrow, inv_count)


def solution(mesh):
    sizes = tuple(mesh.shape[name] for name in ("dp", "ctx", "feat"))
    in_specs = (P(("dp", "ctx"), "feat"), P(("dp", "ctx"), "feat"), P(("dp", "ctx")), P())
    out_specs = (P(("dp", "ctx"), "feat"), P(("dp", "ctx"), "feat"))
    return jax.shard_map(
        functools.partial(local, sizes), mesh=mesh, in_specs=in_specs, out_specs=out_specs, check_vma=False)
```

```python
import functools

import jax
import jax.numpy as jnp
from jax import lax
from jax.experimental import pallas as pl
from jax.experimental.pallas import tpu as pltpu
from jax.sharding import PartitionSpec as P

MESH = pl.DeviceIdType.MESH
LANES = 128
VMEM_LIMIT = 56 * 1024 * 1024


def gather_kernel(sizes, pieces, grads_ref, acts_ref, scale_ref, weighted_ref, turned_ref,
                  cols_ref, rows_ref, swap_send, swap_recv, down_send, up_send, flow_recv,
                  side_send, side_recv):
    n_dp, n_ctx, n_feat = sizes
    group = n_dp * n_ctx
    ratio = n_feat // group
    tokens, wide = grads_ref.shape
    width = wide + acts_ref.shape[1]
    row_step, col_step = tokens // pieces, width // pieces
    steps = group * pieces

    dp, ctx, feat = lax.axis_index("dp"), lax.axis_index("ctx"), lax.axis_index("feat")
    me = dp * n_ctx + ctx
    stage, lane = feat // ratio, feat % ratio

    def in_group(other):
        return {"dp": other // n_ctx, "ctx": other % n_ctx, "feat": feat}

    def on_feat(other):
        return {"dp": dp, "ctx": ctx, "feat": other}

    mates = [lax.rem(me + shift, group) for shift in range(1, group)]
    sides = [stage * ratio + lax.rem(lane + shift, ratio) for shift in range(1, ratio)]
    has_down, has_up = stage > 0, stage < group - 1

    my_start = pl.multiple_of(me * tokens, tokens)
    my_rows = cols_ref.at[pl.ds(my_start, tokens)]
    cols_ref[pl.ds(my_start, tokens), pl.ds(0, wide)] = grads_ref[...]
    cols_ref[pl.ds(my_start, tokens), pl.ds(wide, width - wide)] = acts_ref[...]
    cols_ref[pl.ds(my_start, tokens), pl.ds(width, LANES)] = scale_ref[...]

    barrier = pltpu.get_barrier_semaphore()
    for mate in mates:
        pl.semaphore_signal(barrier, inc=1, device_id=in_group(mate), device_id_type=MESH)
    for side in sides:
        pl.semaphore_signal(barrier, inc=1, device_id=on_feat(side), device_id_type=MESH)

    @pl.when(has_down)
    def _():
        pl.semaphore_signal(barrier, inc=1, device_id=on_feat(feat - ratio), device_id_type=MESH)

    @pl.when(has_up)
    def _():
        pl.semaphore_signal(barrier, inc=1, device_id=on_feat(feat + ratio), device_id_type=MESH)

    near = has_down.astype(jnp.int32) + has_up.astype(jnp.int32)
    pl.semaphore_wait(barrier, len(mates) + len(sides) + near)

    def swap(shift):
        return pltpu.make_async_remote_copy(
            src_ref=my_rows, dst_ref=my_rows,
            send_sem=swap_send.at[shift], recv_sem=swap_recv.at[group - shift],
            device_id=in_group(lax.rem(me + shift, group)), device_id_type=MESH)

    def swapped(shift):
        block = lax.rem(me + shift, group)
        rows = cols_ref.at[pl.ds(pl.multiple_of(block * tokens, tokens), tokens)]
        return pltpu.make_async_remote_copy(
            src_ref=my_rows, dst_ref=rows,
            send_sem=swap_send.at[shift], recv_sem=swap_recv.at[shift],
            device_id=in_group(block), device_id_type=MESH)

    half = group // 2
    order = [(k % 2) * half + k // 2 for k in range(group)] if group % 2 == 0 else list(range(group))
    for shift in order[1:]:
        swap(shift).start()

    is_root = stage == me
    is_flow = jnp.logical_not(is_root)
    send_down = jnp.logical_and(stage <= me, has_down)
    send_up = jnp.logical_and(stage >= me, has_up)

    def block_of(k):
        shift = (k % 2) * half + k // 2 if group % 2 == 0 else k
        return shift, lax.rem(me + shift, group)

    def span(q):
        shift, block = block_of(q // pieces)
        start = block * tokens + (q % pieces) * row_step
        return pl.ds(pl.multiple_of(start, row_step), row_step)

    def from_root(q):
        return cols_ref.at[span(q), pl.ds(0, width)]

    def landed(q, which):
        return rows_ref.at[which, span(q)]

    def remote(src, q, which, send, recv, target):
        return pltpu.make_async_remote_copy(
            src_ref=src, dst_ref=landed(q, which), send_sem=send, recv_sem=recv,
            device_id=on_feat(target), device_id_type=MESH)

    def send_on(src, q):
        @pl.when(send_down)
        def _():
            remote(src, q, lane, down_send.at[q], flow_recv.at[q], feat - ratio).start()

        @pl.when(send_up)
        def _():
            remote(src, q, lane, up_send.at[q], flow_recv.at[q], feat + ratio).start()

        for i, side in enumerate(sides):
            remote(src, q, lane, side_send.at[i, q], side_recv.at[ratio - 2 - i, q], side).start()

    def turn(src_ref, which, block, part):
        at = pl.ds(pl.multiple_of(block * tokens, tokens), tokens)
        start = pl.multiple_of(part * col_step, LANES)
        if src_ref is cols_ref:
            piece = src_ref[at, pl.ds(start, col_step)]
        else:
            piece = src_ref[which, at, pl.ds(start, col_step)]
        out = pl.ds(pl.multiple_of(which * width + start, LANES), col_step)
        turned_ref[out, at] = piece.T

    def finish(k, part):
        shift, block = block_of(k)

        @pl.when(jnp.logical_and(is_flow, jnp.logical_and(part == 0, k > 0)))
        def _():
            swapped(shift).wait_recv()

        at = pl.ds(pl.multiple_of(block * tokens + part * row_step, row_step), row_step)
        scale = cols_ref[at, pl.ds(width, LANES)].astype(jnp.float32)[:, :1]
        weighted_ref[at, :] = (cols_ref[at, pl.ds(0, width)].astype(jnp.float32) * scale).astype(jnp.bfloat16)

        @pl.when(is_root)
        def _():
            turn(cols_ref, lane, block, part)

        @pl.when(is_flow)
        def _():
            turn(rows_ref, lane, block, part)

        for i in range(ratio - 1):
            other = lax.rem(lane + i + 1, ratio)

            @pl.when(part == 0)
            def _():
                def arrive(j, carry):
                    q = k * pieces + j
                    remote(landed(q, other), q, other, side_send.at[i, q], side_recv.at[i, q], feat).wait_recv()
                    return carry

                lax.fori_loop(0, pieces, arrive, 0)

            turn(rows_ref, other, block, part)

    def body(q, carry):
        k, part = q // pieces, q % pieces

        @pl.when(is_root)
        def _():
            @pl.when(jnp.logical_and(part == 0, k > 0))
            def _():
                shift, _ = block_of(k)
                swapped(shift).wait_recv()

            send_on(from_root(q), q)

        @pl.when(is_flow)
        def _():
            remote(landed(q, lane), q, lane, down_send.at[q], flow_recv.at[q], feat).wait_recv()
            send_on(landed(q, lane), q)

        @pl.when(k > 0)
        def _():
            finish(k - 1, part)

        return carry

    lax.fori_loop(0, steps, body, 0)

    def last(part, carry):
        finish(group - 1, part)
        return carry

    lax.fori_loop(0, pieces, last, 0)

    def drain(q, carry):
        here = landed(q, lane)
        for i in range(ratio - 1):
            remote(here, q, lane, side_send.at[i, q], side_recv.at[i, q], feat).wait_send()

        @pl.when(send_down)
        def _():
            remote(here, q, lane, down_send.at[q], flow_recv.at[q], feat).wait_send()

        @pl.when(send_up)
        def _():
            remote(here, q, lane, up_send.at[q], flow_recv.at[q], feat).wait_send()

        return carry

    lax.fori_loop(0, steps, drain, 0)
    for shift in order[1:]:
        swap(shift).wait_send()


def gather_tiles(grads, acts, scale, sizes):
    n_dp, n_ctx, n_feat = sizes
    group = n_dp * n_ctx
    ratio = n_feat // group
    tokens, wide = grads.shape
    width = wide + acts.shape[1]
    pieces = next(p for p in (4, 2, 1) if width % (p * LANES) == 0)
    steps = group * pieces
    dma = pltpu.SemaphoreType.DMA
    vmem = pl.BlockSpec(memory_space=pltpu.VMEM)
    return pl.pallas_call(
        functools.partial(gather_kernel, sizes, pieces),
        out_shape=(
            jax.ShapeDtypeStruct((group * tokens, width), grads.dtype),
            jax.ShapeDtypeStruct((ratio * width, group * tokens), grads.dtype),
        ),
        in_specs=[vmem] * 3,
        out_specs=(vmem, vmem),
        scratch_shapes=[
            pltpu.VMEM((group * tokens, width + LANES), grads.dtype),
            pltpu.VMEM((ratio, group * tokens, width), grads.dtype),
            dma((group,)), dma((group,)),
            dma((steps,)), dma((steps,)), dma((steps,)),
            dma((max(ratio - 1, 1), steps)), dma((max(ratio - 1, 1), steps)),
        ],
        compiler_params=pltpu.CompilerParams(
            collective_id=0, has_side_effects=True, vmem_limit_bytes=VMEM_LIMIT),
        name="gather_tiles",
    )(grads, acts, scale)


def gram_kernel(grad_steps, wide, inv_count, weighted_ref, turned_ref, grad_ref, act_ref):
    step = pl.program_id(0)
    tile = grad_ref.shape[0]

    def tiles(out_ref, offset):
        chunk = tile if out_ref.shape[1] % tile == 0 else LANES
        for n in range(out_ref.shape[1] // chunk):
            total = jnp.dot(turned_ref[...], weighted_ref[:, pl.ds(offset + n * chunk, chunk)],
                            preferred_element_type=jnp.float32)
            out_ref[:, pl.ds(n * chunk, chunk)] = (total * inv_count).astype(jnp.bfloat16)

    @pl.when(step < grad_steps)
    def _():
        tiles(grad_ref, 0)

    @pl.when(step >= grad_steps)
    def _():
        tiles(act_ref, wide)


def gram(weighted, turned, wide, narrow, inv_count):
    tokens, both = weighted.shape
    ratio = turned.shape[0] // both
    tile = next(t for t in (512, 256, 128) if wide % t == 0 and narrow % t == 0)
    grad_tiles, act_tiles = wide // tile, narrow // tile
    grad_steps, act_steps = ratio * grad_tiles, ratio * act_tiles
    lane_tiles = grad_tiles + act_tiles

    def row_block(i):
        j = jnp.maximum(i - grad_steps, 0)
        late = i >= grad_steps
        return (jnp.where(late, (j // act_tiles) * lane_tiles + grad_tiles + j % act_tiles,
                          (i // grad_tiles) * lane_tiles + i % grad_tiles), 0)

    return pl.pallas_call(
        functools.partial(gram_kernel, grad_steps, wide, inv_count),
        grid=(grad_steps + act_steps,),
        out_shape=(
            jax.ShapeDtypeStruct((ratio * wide, wide), jnp.bfloat16),
            jax.ShapeDtypeStruct((ratio * narrow, narrow), jnp.bfloat16),
        ),
        in_specs=[
            pl.BlockSpec((tokens, both), lambda i: (0, 0)),
            pl.BlockSpec((tile, tokens), row_block),
        ],
        out_specs=(
            pl.BlockSpec((tile, wide), lambda i: (jnp.minimum(i, grad_steps - 1), 0)),
            pl.BlockSpec((tile, narrow), lambda i: (jnp.maximum(i - grad_steps, 0), 0)),
        ),
        compiler_params=pltpu.CompilerParams(vmem_limit_bytes=VMEM_LIMIT),
        cost_estimate=pl.CostEstimate(
            flops=2 * tokens * ratio * (wide * wide + narrow * narrow),
            bytes_accessed=2 * (ratio * (wide * wide + narrow * narrow) + turned.size + weighted.size),
            transcendentals=0),
        name="gram",
    )(weighted, turned)


def local(sizes, out_grads, acts, domain_ids, domain_weights):
    tokens, wide = out_grads.shape
    narrow = acts.shape[1]
    inv_count = 1.0 / (tokens * sizes[0] * sizes[1])
    labels = jnp.arange(domain_weights.shape[0], dtype=jnp.int32)
    match = domain_ids[:, None] == labels[None, :]
    weight = jnp.sum(jnp.where(match, domain_weights[None, :], 0), axis=1).astype(jnp.bfloat16)
    scale = jnp.broadcast_to(weight[:, None], (tokens, LANES))
    weighted, turned = gather_tiles(out_grads, acts, scale, sizes)
    return gram(weighted, turned, wide, narrow, inv_count)


def solution(mesh):
    sizes = tuple(mesh.shape[name] for name in ("dp", "ctx", "feat"))
    in_specs = (P(("dp", "ctx"), "feat"), P(("dp", "ctx"), "feat"), P(("dp", "ctx")), P())
    out_specs = (P(("dp", "ctx"), "feat"), P(("dp", "ctx"), "feat"))
    return jax.shard_map(
        functools.partial(local, sizes), mesh=mesh, in_specs=in_specs, out_specs=out_specs, check_vma=False)
```

```python
import functools

import jax
import jax.numpy as jnp
from jax import lax
from jax.experimental import pallas as pl
from jax.experimental.pallas import tpu as pltpu
from jax.sharding import PartitionSpec as P

MESH = pl.DeviceIdType.MESH
LANES = 128
LAG = 2
VMEM_LIMIT = 56 * 1024 * 1024


def gather_kernel(sizes, pieces, grads_ref, acts_ref, scale_ref, weighted_out, turned_out,
                  cols_ref, rows_ref, weighted_ref, turned_ref, weighted_sem, turned_sem, swap_send, swap_recv, down_send, up_send, flow_recv,
                  side_send, side_recv):
    n_dp, n_ctx, n_feat = sizes
    group = n_dp * n_ctx
    ratio = n_feat // group
    tokens, wide = grads_ref.shape
    width = wide + acts_ref.shape[1]
    col_step = width // pieces
    steps = group * pieces

    dp, ctx, feat = lax.axis_index("dp"), lax.axis_index("ctx"), lax.axis_index("feat")
    me = dp * n_ctx + ctx
    stage, lane = feat // ratio, feat % ratio

    def in_group(other):
        return {"dp": other // n_ctx, "ctx": other % n_ctx, "feat": feat}

    def on_feat(other):
        return {"dp": dp, "ctx": ctx, "feat": other}

    mates = [lax.rem(me + shift, group) for shift in range(1, group)]
    sides = [stage * ratio + lax.rem(lane + shift, ratio) for shift in range(1, ratio)]
    has_down, has_up = stage > 0, stage < group - 1

    my_start = pl.multiple_of(me * tokens, tokens)
    my_rows = cols_ref.at[pl.ds(my_start, tokens)]
    cols_ref[pl.ds(my_start, tokens), pl.ds(0, wide)] = grads_ref[...]
    cols_ref[pl.ds(my_start, tokens), pl.ds(wide, width - wide)] = acts_ref[...]
    cols_ref[pl.ds(my_start, tokens), pl.ds(width, LANES)] = scale_ref[...]

    barrier = pltpu.get_barrier_semaphore()
    for mate in mates:
        pl.semaphore_signal(barrier, inc=1, device_id=in_group(mate), device_id_type=MESH)
    for side in sides:
        pl.semaphore_signal(barrier, inc=1, device_id=on_feat(side), device_id_type=MESH)

    @pl.when(has_down)
    def _():
        pl.semaphore_signal(barrier, inc=1, device_id=on_feat(feat - ratio), device_id_type=MESH)

    @pl.when(has_up)
    def _():
        pl.semaphore_signal(barrier, inc=1, device_id=on_feat(feat + ratio), device_id_type=MESH)

    near = has_down.astype(jnp.int32) + has_up.astype(jnp.int32)
    pl.semaphore_wait(barrier, len(mates) + len(sides) + near)

    def swap(shift):
        return pltpu.make_async_remote_copy(
            src_ref=my_rows, dst_ref=my_rows,
            send_sem=swap_send.at[shift], recv_sem=swap_recv.at[group - shift],
            device_id=in_group(lax.rem(me + shift, group)), device_id_type=MESH)

    def swapped(shift):
        block = lax.rem(me + shift, group)
        rows = cols_ref.at[pl.ds(pl.multiple_of(block * tokens, tokens), tokens)]
        return pltpu.make_async_remote_copy(
            src_ref=my_rows, dst_ref=rows,
            send_sem=swap_send.at[shift], recv_sem=swap_recv.at[shift],
            device_id=in_group(block), device_id_type=MESH)

    half = group // 2
    order = [(k % 2) * half + k // 2 for k in range(group)] if group % 2 == 0 else list(range(group))
    for shift in order[1:]:
        swap(shift).start()

    is_root = stage == me
    is_flow = jnp.logical_not(is_root)
    send_down = jnp.logical_and(stage <= me, has_down)
    send_up = jnp.logical_and(stage >= me, has_up)

    def block_of(k):
        shift = (k % 2) * half + k // 2 if group % 2 == 0 else k
        return shift, lax.rem(me + shift, group)

    def span(q):
        _, block = block_of(q // pieces)
        return pl.ds(pl.multiple_of(block * tokens, tokens), tokens)

    def part_of(q):
        return pl.ds(pl.multiple_of((q % pieces) * col_step, LANES), col_step)

    def from_root(q):
        return cols_ref.at[span(q), part_of(q)]

    def landed(q, which):
        return rows_ref.at[which, span(q), part_of(q)]

    def remote(src, q, which, send, recv, target):
        return pltpu.make_async_remote_copy(
            src_ref=src, dst_ref=landed(q, which), send_sem=send, recv_sem=recv,
            device_id=on_feat(target), device_id_type=MESH)

    def send_on(src, q):
        @pl.when(send_down)
        def _():
            remote(src, q, lane, down_send.at[q], flow_recv.at[q], feat - ratio).start()

        @pl.when(send_up)
        def _():
            remote(src, q, lane, up_send.at[q], flow_recv.at[q], feat + ratio).start()

        for i, side in enumerate(sides):
            remote(src, q, lane, side_send.at[i, q], side_recv.at[ratio - 2 - i, q], side).start()

    def turned_copy(q, which, slot):
        start = which * width + (q % pieces) * col_step
        at = (pl.ds(pl.multiple_of(start, LANES), col_step), span(q))
        return pltpu.make_async_copy(turned_ref.at[at], turned_out.at[at], turned_sem.at[slot, q])

    def weighted_copy(q):
        at = (span(q), part_of(q))
        return pltpu.make_async_copy(weighted_ref.at[at], weighted_out.at[at], weighted_sem.at[q])

    def turn(piece, q, which, slot):
        start = which * width + (q % pieces) * col_step
        turned_ref[pl.ds(pl.multiple_of(start, LANES), col_step), span(q)] = piece.T
        turned_copy(q, which, slot).start()

    def finish(q):
        k, part = q // pieces, q % pieces
        shift, _ = block_of(k)

        @pl.when(jnp.logical_and(is_flow, jnp.logical_and(part == 0, k > 0)))
        def _():
            swapped(shift).wait_recv()

        @pl.when(is_root)
        def _():
            turn(cols_ref[span(q), part_of(q)], q, lane, 0)

        @pl.when(is_flow)
        def _():
            turn(rows_ref[lane, span(q), part_of(q)], q, lane, 0)

        scale = cols_ref[span(q), pl.ds(width, LANES)].astype(jnp.float32)[:, :1]
        weighted_ref[span(q), part_of(q)] = (
            cols_ref[span(q), part_of(q)].astype(jnp.float32) * scale).astype(jnp.bfloat16)
        weighted_copy(q).start()

        for i in range(ratio - 1):
            other = lax.rem(lane + i + 1, ratio)
            remote(landed(q, other), q, other, side_send.at[i, q], side_recv.at[i, q], feat).wait_recv()
            turn(rows_ref[other, span(q), part_of(q)], q, other, 1 + i)

    def body(q, carry):
        k, part = q // pieces, q % pieces

        @pl.when(is_root)
        def _():
            @pl.when(jnp.logical_and(part == 0, k > 0))
            def _():
                shift, _ = block_of(k)
                swapped(shift).wait_recv()

            send_on(from_root(q), q)

        @pl.when(is_flow)
        def _():
            remote(landed(q, lane), q, lane, down_send.at[q], flow_recv.at[q], feat).wait_recv()
            send_on(landed(q, lane), q)

        @pl.when(q >= LAG)
        def _():
            finish(q - LAG)

        return carry

    lax.fori_loop(0, steps, body, 0)

    def last(q, carry):
        finish(q)
        return carry

    lax.fori_loop(steps - LAG, steps, last, 0)

    def drain(q, carry):
        here = landed(q, lane)
        turned_copy(q, lane, 0).wait()
        weighted_copy(q).wait()
        for i in range(ratio - 1):
            other = lax.rem(lane + i + 1, ratio)
            remote(here, q, lane, side_send.at[i, q], side_recv.at[i, q], feat).wait_send()
            turned_copy(q, other, 1 + i).wait()

        @pl.when(send_down)
        def _():
            remote(here, q, lane, down_send.at[q], flow_recv.at[q], feat).wait_send()

        @pl.when(send_up)
        def _():
            remote(here, q, lane, up_send.at[q], flow_recv.at[q], feat).wait_send()

        return carry

    lax.fori_loop(0, steps, drain, 0)
    for shift in order[1:]:
        swap(shift).wait_send()


def gather_tiles(grads, acts, scale, sizes):
    n_dp, n_ctx, n_feat = sizes
    group = n_dp * n_ctx
    ratio = n_feat // group
    tokens, wide = grads.shape
    width = wide + acts.shape[1]
    pieces = next(p for p in (9, 6, 4, 3, 2, 1) if width % (p * LANES) == 0)
    steps = group * pieces
    dma = pltpu.SemaphoreType.DMA
    vmem = pl.BlockSpec(memory_space=pltpu.VMEM)
    return pl.pallas_call(
        functools.partial(gather_kernel, sizes, pieces),
        out_shape=(
            jax.ShapeDtypeStruct((group * tokens, width), grads.dtype),
            jax.ShapeDtypeStruct((ratio * width, group * tokens), grads.dtype),
        ),
        in_specs=[vmem] * 3,
        out_specs=(pl.BlockSpec(memory_space=pl.ANY), pl.BlockSpec(memory_space=pl.ANY)),
        scratch_shapes=[
            pltpu.VMEM((group * tokens, width + LANES), grads.dtype),
            pltpu.VMEM((ratio, group * tokens, width), grads.dtype),
            pltpu.VMEM((group * tokens, width), grads.dtype),
            pltpu.VMEM((ratio * width, group * tokens), grads.dtype),
            dma((steps,)), dma((ratio, steps)),
            dma((group,)), dma((group,)),
            dma((steps,)), dma((steps,)), dma((steps,)),
            dma((max(ratio - 1, 1), steps)), dma((max(ratio - 1, 1), steps)),
        ],
        compiler_params=pltpu.CompilerParams(
            collective_id=0, has_side_effects=True, vmem_limit_bytes=VMEM_LIMIT),
        name="gather_tiles",
    )(grads, acts, scale)


def gram_kernel(lane_steps, grad_steps, inv_count, weighted_ref, turned_ref, grad_ref, act_ref):
    step = pl.program_id(0) % lane_steps
    wide = grad_ref.shape[0]
    tile = weighted_ref.shape[1]
    chunk = min(tile, 256)

    def fill(out_ref, start):
        height = next(h for h in (1792, 1024, 512, 256, 128) if out_ref.shape[0] % h == 0)
        for n in range(tile // chunk):
            for m in range(out_ref.shape[0] // height):
                total = jnp.dot(turned_ref[pl.ds(start + m * height, height), :],
                                weighted_ref[:, pl.ds(n * chunk, chunk)],
                                preferred_element_type=jnp.float32)
                out_ref[pl.ds(m * height, height), pl.ds(n * chunk, chunk)] = (
                    total * inv_count).astype(jnp.bfloat16)

    @pl.when(step < grad_steps)
    def _():
        fill(grad_ref, 0)

    @pl.when(step >= grad_steps)
    def _():
        fill(act_ref, wide)


def gram(weighted, turned, wide, narrow, inv_count):
    tokens, both = weighted.shape
    ratio = turned.shape[0] // both
    tile = next(t for t in (512, 256, 128) if wide % t == 0 and narrow % t == 0)
    grad_steps, act_steps = wide // tile, narrow // tile
    lane_steps = grad_steps + act_steps

    def grad_block(i):
        return i // lane_steps, jnp.minimum(i % lane_steps, grad_steps - 1)

    def act_block(i):
        lane, step = i // lane_steps, i % lane_steps
        early = step < grad_steps
        return (jnp.where(early, jnp.maximum(lane - 1, 0), lane),
                jnp.where(early, jnp.where(lane > 0, act_steps - 1, 0), step - grad_steps))

    return pl.pallas_call(
        functools.partial(gram_kernel, lane_steps, grad_steps, inv_count),
        grid=(ratio * lane_steps,),
        out_shape=(
            jax.ShapeDtypeStruct((ratio * wide, wide), jnp.bfloat16),
            jax.ShapeDtypeStruct((ratio * narrow, narrow), jnp.bfloat16),
        ),
        in_specs=[
            pl.BlockSpec((tokens, tile), lambda i: (0, i % lane_steps)),
            pl.BlockSpec((both, tokens), lambda i: (i // lane_steps, 0)),
        ],
        out_specs=(
            pl.BlockSpec((wide, tile), grad_block),
            pl.BlockSpec((narrow, tile), act_block),
        ),
        compiler_params=pltpu.CompilerParams(vmem_limit_bytes=VMEM_LIMIT),
        cost_estimate=pl.CostEstimate(
            flops=2 * tokens * ratio * (wide * wide + narrow * narrow),
            bytes_accessed=2 * (ratio * (wide * wide + narrow * narrow) + turned.size + weighted.size),
            transcendentals=0),
        name="gram",
    )(weighted, turned)


def local(sizes, out_grads, acts, domain_ids, domain_weights):
    tokens, wide = out_grads.shape
    narrow = acts.shape[1]
    inv_count = 1.0 / (tokens * sizes[0] * sizes[1])
    labels = jnp.arange(domain_weights.shape[0], dtype=jnp.int32)
    match = domain_ids[:, None] == labels[None, :]
    weight = jnp.sum(jnp.where(match, domain_weights[None, :], 0), axis=1).astype(jnp.bfloat16)
    scale = jnp.broadcast_to(weight[:, None], (tokens, LANES))
    weighted, turned = gather_tiles(out_grads, acts, scale, sizes)
    return gram(weighted, turned, wide, narrow, inv_count)


def solution(mesh):
    sizes = tuple(mesh.shape[name] for name in ("dp", "ctx", "feat"))
    in_specs = (P(("dp", "ctx"), "feat"), P(("dp", "ctx"), "feat"), P(("dp", "ctx")), P())
    out_specs = (P(("dp", "ctx"), "feat"), P(("dp", "ctx"), "feat"))
    return jax.shard_map(
        functools.partial(local, sizes), mesh=mesh, in_specs=in_specs, out_specs=out_specs, check_vma=False)
```

```python
import functools

import jax
import jax.numpy as jnp
from jax import lax
from jax.experimental import pallas as pl
from jax.experimental.pallas import tpu as pltpu
from jax.sharding import PartitionSpec as P

MESH = pl.DeviceIdType.MESH
LANES = 128
LAG = 2
VMEM_LIMIT = 56 * 1024 * 1024


def gather_kernel(sizes, pieces, grads_ref, acts_ref, scale_ref, weighted_out, turned_out,
                  cols_ref, rows_ref, weighted_ref, turned_ref, weighted_sem, turned_sem, swap_send, swap_recv, down_send, up_send, flow_recv,
                  side_send, side_recv):
    n_dp, n_ctx, n_feat = sizes
    group = n_dp * n_ctx
    ratio = n_feat // group
    tokens, wide = grads_ref.shape
    width = wide + acts_ref.shape[1]
    col_step = width // pieces
    steps = group * pieces

    dp, ctx, feat = lax.axis_index("dp"), lax.axis_index("ctx"), lax.axis_index("feat")
    me = dp * n_ctx + ctx
    stage, lane = feat // ratio, feat % ratio

    def in_group(other):
        return {"dp": other // n_ctx, "ctx": other % n_ctx, "feat": feat}

    def on_feat(other):
        return {"dp": dp, "ctx": ctx, "feat": other}

    mates = [lax.rem(me + shift, group) for shift in range(1, group)]
    sides = [stage * ratio + lax.rem(lane + shift, ratio) for shift in range(1, ratio)]
    has_down, has_up = stage > 0, stage < group - 1

    my_start = pl.multiple_of(me * tokens, tokens)
    my_rows = cols_ref.at[pl.ds(my_start, tokens)]
    cols_ref[pl.ds(my_start, tokens), pl.ds(0, wide)] = grads_ref[...]
    cols_ref[pl.ds(my_start, tokens), pl.ds(wide, width - wide)] = acts_ref[...]
    cols_ref[pl.ds(my_start, tokens), pl.ds(width, LANES)] = scale_ref[...]

    barrier = pltpu.get_barrier_semaphore()
    for mate in mates:
        pl.semaphore_signal(barrier, inc=1, device_id=in_group(mate), device_id_type=MESH)
    for side in sides:
        pl.semaphore_signal(barrier, inc=1, device_id=on_feat(side), device_id_type=MESH)

    @pl.when(has_down)
    def _():
        pl.semaphore_signal(barrier, inc=1, device_id=on_feat(feat - ratio), device_id_type=MESH)

    @pl.when(has_up)
    def _():
        pl.semaphore_signal(barrier, inc=1, device_id=on_feat(feat + ratio), device_id_type=MESH)

    near = has_down.astype(jnp.int32) + has_up.astype(jnp.int32)
    pl.semaphore_wait(barrier, len(mates) + len(sides) + near)

    def swap(shift):
        return pltpu.make_async_remote_copy(
            src_ref=my_rows, dst_ref=my_rows,
            send_sem=swap_send.at[shift], recv_sem=swap_recv.at[group - shift],
            device_id=in_group(lax.rem(me + shift, group)), device_id_type=MESH)

    def swapped(shift):
        block = lax.rem(me + shift, group)
        rows = cols_ref.at[pl.ds(pl.multiple_of(block * tokens, tokens), tokens)]
        return pltpu.make_async_remote_copy(
            src_ref=my_rows, dst_ref=rows,
            send_sem=swap_send.at[shift], recv_sem=swap_recv.at[shift],
            device_id=in_group(block), device_id_type=MESH)

    half = group // 2
    order = [(k % 2) * half + k // 2 for k in range(group)] if group % 2 == 0 else list(range(group))
    for shift in order[1:]:
        swap(shift).start()

    is_root = stage == me
    is_flow = jnp.logical_not(is_root)
    send_down = jnp.logical_and(stage <= me, has_down)
    send_up = jnp.logical_and(stage >= me, has_up)

    def block_of(k):
        shift = (k % 2) * half + k // 2 if group % 2 == 0 else k
        return shift, lax.rem(me + shift, group)

    def span(q):
        _, block = block_of(q // pieces)
        return pl.ds(pl.multiple_of(block * tokens, tokens), tokens)

    def part_of(q):
        return pl.ds(pl.multiple_of((q % pieces) * col_step, LANES), col_step)

    def from_root(q):
        return cols_ref.at[span(q), part_of(q)]

    def landed(q, which):
        return rows_ref.at[which, span(q), part_of(q)]

    def remote(src, q, which, send, recv, target):
        return pltpu.make_async_remote_copy(
            src_ref=src, dst_ref=landed(q, which), send_sem=send, recv_sem=recv,
            device_id=on_feat(target), device_id_type=MESH)

    def send_on(src, q):
        @pl.when(send_down)
        def _():
            remote(src, q, lane, down_send.at[q], flow_recv.at[q], feat - ratio).start()

        @pl.when(send_up)
        def _():
            remote(src, q, lane, up_send.at[q], flow_recv.at[q], feat + ratio).start()

        for i, side in enumerate(sides):
            remote(src, q, lane, side_send.at[i, q], side_recv.at[ratio - 2 - i, q], side).start()

    def turned_copy(q, which, slot):
        start = which * width + (q % pieces) * col_step
        at = (pl.ds(pl.multiple_of(start, LANES), col_step), span(q))
        return pltpu.make_async_copy(turned_ref.at[at], turned_out.at[at], turned_sem.at[slot, q])

    def weighted_copy(q):
        at = (span(q), part_of(q))
        return pltpu.make_async_copy(weighted_ref.at[at], weighted_out.at[at], weighted_sem.at[q])

    def turn(piece, q, which, slot):
        start = which * width + (q % pieces) * col_step
        turned_ref[pl.ds(pl.multiple_of(start, LANES), col_step), span(q)] = piece.T
        turned_copy(q, which, slot).start()

    def finish(q):
        k, part = q // pieces, q % pieces
        shift, _ = block_of(k)

        @pl.when(jnp.logical_and(is_flow, jnp.logical_and(part == 0, k > 0)))
        def _():
            swapped(shift).wait_recv()

        @pl.when(is_root)
        def _():
            turn(cols_ref[span(q), part_of(q)], q, lane, 0)

        @pl.when(is_flow)
        def _():
            turn(rows_ref[lane, span(q), part_of(q)], q, lane, 0)

        scale = cols_ref[span(q), pl.ds(width, LANES)].astype(jnp.float32)[:, :1]
        weighted_ref[span(q), part_of(q)] = (
            cols_ref[span(q), part_of(q)].astype(jnp.float32) * scale).astype(jnp.bfloat16)
        weighted_copy(q).start()

        for i in range(ratio - 1):
            other = lax.rem(lane + i + 1, ratio)
            remote(landed(q, other), q, other, side_send.at[i, q], side_recv.at[i, q], feat).wait_recv()
            turn(rows_ref[other, span(q), part_of(q)], q, other, 1 + i)

    def body(q, carry):
        k, part = q // pieces, q % pieces

        @pl.when(is_root)
        def _():
            @pl.when(jnp.logical_and(part == 0, k > 0))
            def _():
                shift, _ = block_of(k)
                swapped(shift).wait_recv()

            send_on(from_root(q), q)

        @pl.when(is_flow)
        def _():
            remote(landed(q, lane), q, lane, down_send.at[q], flow_recv.at[q], feat).wait_recv()
            send_on(landed(q, lane), q)

        @pl.when(q >= LAG)
        def _():
            finish(q - LAG)

        return carry

    lax.fori_loop(0, steps, body, 0)

    def last(q, carry):
        finish(q)
        return carry

    lax.fori_loop(steps - LAG, steps, last, 0)

    def drain(q, carry):
        here = landed(q, lane)
        turned_copy(q, lane, 0).wait()
        weighted_copy(q).wait()
        for i in range(ratio - 1):
            other = lax.rem(lane + i + 1, ratio)
            remote(here, q, lane, side_send.at[i, q], side_recv.at[i, q], feat).wait_send()
            turned_copy(q, other, 1 + i).wait()

        @pl.when(send_down)
        def _():
            remote(here, q, lane, down_send.at[q], flow_recv.at[q], feat).wait_send()

        @pl.when(send_up)
        def _():
            remote(here, q, lane, up_send.at[q], flow_recv.at[q], feat).wait_send()

        return carry

    lax.fori_loop(0, steps, drain, 0)
    for shift in order[1:]:
        swap(shift).wait_send()


def gather_tiles(grads, acts, scale, sizes):
    n_dp, n_ctx, n_feat = sizes
    group = n_dp * n_ctx
    ratio = n_feat // group
    tokens, wide = grads.shape
    width = wide + acts.shape[1]
    pieces = next(p for p in (9, 6, 4, 3, 2, 1) if width % (p * LANES) == 0)
    steps = group * pieces
    dma = pltpu.SemaphoreType.DMA
    vmem = pl.BlockSpec(memory_space=pltpu.VMEM)
    return pl.pallas_call(
        functools.partial(gather_kernel, sizes, pieces),
        out_shape=(
            jax.ShapeDtypeStruct((group * tokens, width), grads.dtype),
            jax.ShapeDtypeStruct((ratio * width, group * tokens), grads.dtype),
        ),
        in_specs=[vmem] * 3,
        out_specs=(pl.BlockSpec(memory_space=pl.ANY), pl.BlockSpec(memory_space=pl.ANY)),
        scratch_shapes=[
            pltpu.VMEM((group * tokens, width + LANES), grads.dtype),
            pltpu.VMEM((ratio, group * tokens, width), grads.dtype),
            pltpu.VMEM((group * tokens, width), grads.dtype),
            pltpu.VMEM((ratio * width, group * tokens), grads.dtype),
            dma((steps,)), dma((ratio, steps)),
            dma((group,)), dma((group,)),
            dma((steps,)), dma((steps,)), dma((steps,)),
            dma((max(ratio - 1, 1), steps)), dma((max(ratio - 1, 1), steps)),
        ],
        compiler_params=pltpu.CompilerParams(
            collective_id=0, has_side_effects=True, vmem_limit_bytes=VMEM_LIMIT),
        name="gather_tiles",
    )(grads, acts, scale)


def gram_kernel(grad_steps, wide, inv_count, weighted_ref, turned_ref, grad_ref, act_ref):
    step = pl.program_id(0)
    tile = grad_ref.shape[0]

    def tiles(out_ref, offset):
        chunk = tile if out_ref.shape[1] % tile == 0 else LANES
        for n in range(out_ref.shape[1] // chunk):
            total = jnp.dot(turned_ref[...], weighted_ref[:, pl.ds(offset + n * chunk, chunk)],
                            preferred_element_type=jnp.float32)
            out_ref[:, pl.ds(n * chunk, chunk)] = (total * inv_count).astype(jnp.bfloat16)

    @pl.when(step < grad_steps)
    def _():
        tiles(grad_ref, 0)

    @pl.when(step >= grad_steps)
    def _():
        tiles(act_ref, wide)


def gram(weighted, turned, wide, narrow, inv_count):
    tokens, both = weighted.shape
    ratio = turned.shape[0] // both
    tile = next(t for t in (512, 256, 128) if wide % t == 0 and narrow % t == 0)
    grad_tiles, act_tiles = wide // tile, narrow // tile
    grad_steps, act_steps = ratio * grad_tiles, ratio * act_tiles
    lane_tiles = grad_tiles + act_tiles

    def row_block(i):
        j = jnp.maximum(i - grad_steps, 0)
        late = i >= grad_steps
        return (jnp.where(late, (j // act_tiles) * lane_tiles + grad_tiles + j % act_tiles,
                          (i // grad_tiles) * lane_tiles + i % grad_tiles), 0)

    return pl.pallas_call(
        functools.partial(gram_kernel, grad_steps, wide, inv_count),
        grid=(grad_steps + act_steps,),
        out_shape=(
            jax.ShapeDtypeStruct((ratio * wide, wide), jnp.bfloat16),
            jax.ShapeDtypeStruct((ratio * narrow, narrow), jnp.bfloat16),
        ),
        in_specs=[
            pl.BlockSpec((tokens, both), lambda i: (0, 0)),
            pl.BlockSpec((tile, tokens), row_block),
        ],
        out_specs=(
            pl.BlockSpec((tile, wide), lambda i: (jnp.minimum(i, grad_steps - 1), 0)),
            pl.BlockSpec((tile, narrow), lambda i: (jnp.maximum(i - grad_steps, 0), 0)),
        ),
        compiler_params=pltpu.CompilerParams(vmem_limit_bytes=VMEM_LIMIT),
        cost_estimate=pl.CostEstimate(
            flops=2 * tokens * ratio * (wide * wide + narrow * narrow),
            bytes_accessed=2 * (ratio * (wide * wide + narrow * narrow) + turned.size + weighted.size),
            transcendentals=0),
        name="gram",
    )(weighted, turned)


def local(sizes, out_grads, acts, domain_ids, domain_weights):
    tokens, wide = out_grads.shape
    narrow = acts.shape[1]
    inv_count = 1.0 / (tokens * sizes[0] * sizes[1])
    labels = jnp.arange(domain_weights.shape[0], dtype=jnp.int32)
    match = domain_ids[:, None] == labels[None, :]
    weight = jnp.sum(jnp.where(match, domain_weights[None, :], 0), axis=1).astype(jnp.bfloat16)
    scale = jnp.broadcast_to(weight[:, None], (tokens, LANES))
    weighted, turned = gather_tiles(out_grads, acts, scale, sizes)
    return gram(weighted, turned, wide, narrow, inv_count)


def solution(mesh):
    sizes = tuple(mesh.shape[name] for name in ("dp", "ctx", "feat"))
    in_specs = (P(("dp", "ctx"), "feat"), P(("dp", "ctx"), "feat"), P(("dp", "ctx")), P())
    out_specs = (P(("dp", "ctx"), "feat"), P(("dp", "ctx"), "feat"))
    return jax.shard_map(
        functools.partial(local, sizes), mesh=mesh, in_specs=in_specs, out_specs=out_specs, check_vma=False)
```
